128 devices in a mesh: tm: 32 (over x_lo, y, z), probe: 4 (over x_hi, core).
Axes of the slice: x: 4 (x_hi: 2, x_lo: 2; x = x_hi * 2 + x_lo), y: 4, z: 4, core: 2. Of those that a mesh axis runs over, the one named last changes fastest.
Arguments:
- raw: float32 [4, 384, 131072], P('probe', 'tm'), may hold values from -8 to 8
- whitening: bfloat16 [4, 384, 384], P('probe'), may hold values from -0.3125 to 0.3125
- taps: float32 [65], replicated, may hold values from -0.75 to 0.75
- temporal: bfloat16 [3, 65], replicated, may hold values from -1.5 to 1.5
- spatial: bfloat16 [4, 3, 256, 384], P('probe'), may hold values from -1.5 to 1.5
- spike_time: int32 [4, 65536], P('probe', 'tm'), may hold values from 0 to 131071, as said below
- spike_template: int32 [4, 65536], P('probe', 'tm'), may hold values from 0 to 255
- spike_amp: bfloat16 [4, 65536], P('probe', 'tm'), may hold values from 1 to 8
Outputs:
- cleaned: float32 [4, 131072, 384], P('probe', 'tm')
The draws below stay inside these ranges and needn't reach their ends.
Inputs may be any that keep to these rules, and one draw needn't show every extreme that they name: `spike_time`: for each probe, slots d * 2048 to (d + 1) * 2048 - 1 hold samples of block d, from d * 4096 to (d + 1) * 4096 - 1.
All inputs are finite; a program needn't handle non-finite values.
Results may differ from the reference program's by a relative error of at most 0.0029.
Values may be sent and summed in bfloat16 or wider, within the bound.
A program may use at most 128 MiB of HBM per device.

```python
import math
import jax
import jax.numpy as jnp
import numpy as np
from jax import lax

PCH = 384
NTEMP = 256
RANK = 3
TW = 65
NTAP = 65
TCH = 4096
PROBES = 4
HW = 32
HALF = 32
NSP = 2048
SAMPLES = 131072
SPIKES = 65536


def draw_spike_time(key, part):
    key = jax.random.fold_in(key, 11)
    offsets = jax.random.randint(key, (PROBES, SPIKES), 0, TCH)
    blocks = jnp.arange(SPIKES, dtype=jnp.int32) // NSP
    times = blocks[None, :] * TCH + offsets
    times = times.at[:, 0].set(0).at[:, SPIKES - 1].set(SAMPLES - 1)
    return times.astype(jnp.int32)


def plant(values, rng, least, high):
    longest = values.shape.index(max(values.shape))
    spots = []
    for shift in (0, 1):
        where = [jax.random.randint(jax.random.fold_in(rng, axis), (), 0, length) for axis, length in enumerate(values.shape)]
        where[longest] = (where[longest] + shift) % values.shape[longest]
        spots.append(tuple(where))
    return values.at[spots[0]].set(least).at[spots[1]].set(high)


def shard_levels(own_key, shape, shards, least, high):
    level = 1.0
    for axis_at, shards_of in shards:
        draws = jax.random.uniform(jax.random.fold_in(jax.random.fold_in(own_key, 6), axis_at), (shards_of,), jnp.float32, least / len(shards), high / len(shards))
        level = level * jnp.repeat(jnp.exp(draws), shape[axis_at] // shards_of).reshape((-1,) + (1,) * (len(shape) - 1 - axis_at))
    return level


def rank_table(number_of, lean):
    weights = [(1 << 20) // math.isqrt(rank ** lean) + 1 for rank in range(1, number_of + 1)]
    scale = 1 + sum(weights) // (1 << 30)
    return np.cumsum(np.array([max(1, weight // scale) for weight in weights]))


def skewed_ids(rng, extent, amount, skew):
    listing = rank_table(amount, skew)
    lot = jax.random.randint(jax.random.fold_in(rng, 1), extent, 0, int(listing[amount - 1]))
    rank = jnp.searchsorted(jnp.asarray(listing, jnp.int32), lot, side="right")
    return jax.random.permutation(jax.random.fold_in(rng, 2), amount)[rank].astype(jnp.int32)


def scatter_about(stream_key, extent, spread, most, cuts=(), held_as=jnp.bfloat16):
    loudness = shard_levels(stream_key, extent, cuts, -0.22, 0.18) if cuts else 1.0
    array = jax.random.normal(stream_key, extent, jnp.float32) * spread * loudness
    return jnp.minimum(jnp.maximum(array, -most), most).astype(held_as)


def setup_inputs(seed: int = 0) -> dict:
    arg_keys = jax.random.split(jax.random.key(seed), 9)
    return {
        "raw": scatter_about(arg_keys[0], (PROBES, PCH, SAMPLES), 1.0, 8.0, ((0, 4), (1, 32)), jnp.float32),
        "whitening": scatter_about(arg_keys[1], (PROBES, PCH, PCH), PCH ** -0.5, 0.3125, ((0, 4),)),
        "taps": scatter_about(arg_keys[2], (NTAP,), NTAP ** -0.5, 0.75, (), jnp.float32),
        "temporal": scatter_about(arg_keys[3], (RANK, TW), 0.25, 1.5),
        "spatial": scatter_about(arg_keys[4], (PROBES, RANK, NTEMP, PCH), 0.25, 1.5, ((0, 4),)),
        "spike_time": draw_spike_time(jax.random.fold_in(arg_keys[8], 71), 0),
        "spike_template": plant(skewed_ids(arg_keys[6], (PROBES, SPIKES), NTEMP, 2), jax.random.fold_in(arg_keys[6], 3), 0, NTEMP - 1).astype(jnp.int32),
        "spike_amp": jnp.clip(jnp.exp(math.log(8.0) - 2.0794415 * jax.random.uniform(arg_keys[7], (PROBES, SPIKES), jnp.float32) ** shard_levels(arg_keys[7], (PROBES, SPIKES), ((0, 4), (1, 32)), -0.2, 0.2)), 1.0, 8.0).astype(jnp.bfloat16),
    }


def band_matrix(taps, rows):
    width = taps.shape[0]
    flat = jnp.concatenate([taps, jnp.zeros((rows,), taps.dtype)])
    tiled = jnp.tile(flat, rows)[: rows * (rows + width - 1)]
    return tiled.reshape(rows, rows + width - 1)


def band_apply(padded, kernels, rows, block, precision):
    width = kernels.shape[1]
    ranks = kernels.shape[0]
    channels = padded.shape[2]
    block = min(block, rows)
    count = rows // block
    bands = jnp.stack([band_matrix(kernels[r], block) for r in range(ranks)], axis=0)
    if count == 1:
        return jnp.einsum("rij,rjc->ic", bands, padded[:, : block + width - 1], precision=precision, preferred_element_type=jnp.float32)
    main_band = bands[:, :, :block]
    tail_band = bands[:, :, block:]
    main = padded[:, :rows].reshape(ranks, count, block, channels)
    inner = padded[:, block:rows].reshape(ranks, count - 1, block, channels)[:, :, : width - 1]
    last = padded[:, rows : rows + width - 1][:, None]
    tails = jnp.concatenate([inner, last], axis=1)
    out = jnp.einsum("rij,rbjc->bic", main_band, main, precision=precision, preferred_element_type=jnp.float32)
    out = out + jnp.einsum("rij,rbjc->bic", tail_band, tails, precision=precision, preferred_element_type=jnp.float32)
    return out.reshape(rows, channels)


def reference(raw, whitening, taps, temporal, spatial, spike_time, spike_template, spike_amp):
    reverse = temporal[:, ::-1]
    outputs = []
    for probe_id in range(PROBES):
        raw_padded = jnp.pad(raw[probe_id], ((0, 0), (HALF, HALF)))
        events = jnp.zeros((SAMPLES, NTEMP), jnp.float32)
        events = events.at[spike_time[probe_id], spike_template[probe_id]].add(spike_amp[probe_id].astype(jnp.float32))
        events = jnp.pad(events.astype(jnp.bfloat16), ((HW, HW), (0, 0)))
        spatial_wide = spatial[probe_id].astype(jnp.float32)
        white_matrix = whitening[probe_id]

        def one_block(index):
            start = (index * TCH).astype(jnp.int32)
            piece = lax.dynamic_slice_in_dim(raw_padded, start, TCH + 2 * HALF, 1)
            white = lax.dot_general(piece.astype(jnp.bfloat16), white_matrix, (((0,), (0,)), ((), ())), preferred_element_type=jnp.float32)
            filtered = band_apply(white[None], taps[None], TCH, 512, lax.Precision.HIGHEST)
            window = lax.dynamic_slice_in_dim(events, start, TCH + 2 * HW, 0)
            loads = jnp.einsum("tk,rkc->rtc", window.astype(jnp.float32), spatial_wide).astype(jnp.bfloat16)
            spill = band_apply(loads, reverse, TCH, 512, None)
            return filtered - spill

        blocks = lax.map(one_block, jnp.arange(SAMPLES // TCH, dtype=jnp.int32))
        outputs.append(blocks.reshape(SAMPLES, PCH))
    return jnp.stack(outputs, axis=0)
```

```python
import jax
import jax.numpy as jnp
from jax import lax
from jax.experimental import pallas as pl
from jax.experimental.pallas import tpu as pltpu
from jax.sharding import PartitionSpec as P

MESH = pl.DeviceIdType.MESH
DEVICES = 32
CH = 12
PCH = 384
NTEMP = 256
RANK = 3
NTAP = 65
TCH = 4096
NSP = 2048
LANE = 128
BLOCKS = TCH // LANE
ROUNDS = 4
PER = BLOCKS // ROUNDS
ROWS = CH * PER
HW = 32
GROUP = 4
STEP = 192
NEAR = (1, 2, 4, 6, 8, 16, 24)
FAR = tuple(k for k in ((j * 11) % DEVICES for j in range(1, DEVICES)) if k not in NEAR)


def partner(me, k):
    x, y, z = me // 16, (me // 4) % 4, me % 4
    x = (x + k % 2) % 2
    y = (y + (k // 2) % 4) % 4
    z = (z + k // 8) % 4
    return x * 16 + y * 4 + z


def kernel(
    raw, white, taps, temporal, spatial, time, tmpl, amp, out,
    wide, lhs, outbox, inbox, hot, picked, events, loads, turned, band, bands, wmat, smat,
    taps_in, temporal_in, time_in, tmpl_in, amp_in, rows,
    raw_sem, mat_sem, send_sem, recv_sem, halo_send, halo_recv, plane_sem, all_sem,
):
    me = lax.axis_index("tm")

    barrier = pltpu.get_barrier_semaphore()
    for k in NEAR:
        pl.semaphore_signal(barrier, inc=1, device_id={"tm": partner(me, k)}, device_id_type=MESH)

    load = pltpu.make_async_copy(raw, wide.at[:, pl.ds(8, TCH * DEVICES // LANE), :], raw_sem)
    load.start()
    small = ((taps, taps_in), (temporal, temporal_in), (time, time_in), (tmpl, tmpl_in), (amp, amp_in))
    gets = [
        pltpu.make_async_copy(there, here, mat_sem.at[i])
        for i, (there, here) in enumerate(small + ((spatial, smat), (white, wmat)))
    ]
    for get in gets:
        get.start()

    edge = jnp.zeros((CH, 8, LANE), jnp.float32)
    wide[:, 0:8, :] = edge
    wide[:, 8 + TCH * DEVICES // LANE : 16 + TCH * DEVICES // LANE, :] = edge

    rows[...] = jnp.zeros((8, 256), jnp.float32)
    gets[0].wait()
    rows[RANK : RANK + 1, 0:NTAP] = taps_in[...]
    gets[1].wait()
    rows[0:RANK, 0:NTAP] = temporal_in[...].astype(jnp.float32)

    fine = rows[RANK : RANK + 1, :]
    coarse = fine.astype(jnp.bfloat16).astype(jnp.float32)
    for i, part in enumerate((coarse, fine - coarse)):
        spread = jnp.broadcast_to(part, (LANE, 256))
        ring = pltpu.roll(spread, 224, 1, stride=1, stride_axis=0)
        band[:, i * LANE : (i + 1) * LANE] = ring.T.astype(jnp.bfloat16)

    load.wait()

    def filter_round(r):
        @pl.loop(0, DEVICES // GROUP)
        def _(g):
            for j in range(GROUP):
                base = pl.multiple_of(8 + partner(me, g * GROUP + j) * BLOCKS + r * PER, 8)
                here = wide[:, pl.ds(base, PER), :]
                behind = wide[:, pl.ds(base - 1, PER), :]
                ahead = wide[:, pl.ds(base + 1, PER), :]
                lane = lax.broadcasted_iota(jnp.int32, here.shape, 2)
                beside = jnp.where(lane < 64, ahead, behind)
                lhs[j * ROWS : (j + 1) * ROWS, :LANE] = here.reshape(ROWS, LANE).astype(jnp.bfloat16)
                lhs[j * ROWS : (j + 1) * ROWS, LANE:] = beside.reshape(ROWS, LANE).astype(jnp.bfloat16)
            both = jnp.dot(lhs[...], band[...], preferred_element_type=jnp.float32)
            done = (both[:, :LANE] + both[:, LANE:]).astype(jnp.bfloat16)
            outbox[r, pl.ds(g * GROUP, GROUP)] = done.reshape(GROUP, ROWS, LANE)

        inbox[r, me] = outbox[r, 0]

    def send(r, k):
        pltpu.make_async_remote_copy(
            src_ref=outbox.at[r, k],
            dst_ref=inbox.at[r, me],
            send_sem=send_sem.at[r],
            recv_sem=recv_sem.at[r],
            device_id={"tm": partner(me, k)},
            device_id_type=MESH,
        ).start()

    filter_round(0)
    pl.semaphore_wait(barrier, len(NEAR))
    for k in (2, 4, 6):
        pl.semaphore_signal(plane_sem, inc=1, device_id={"tm": partner(me, k)}, device_id_type=MESH)
    for k in NEAR:
        send(0, k)
    pl.semaphore_wait(plane_sem, 3)
    pl.semaphore_signal(all_sem, inc=1, device_id={"tm": partner(me, 1)}, device_id_type=MESH)
    pl.semaphore_wait(all_sem, 1)
    for k in FAR:
        send(0, k)

    def send_round(r):
        @pl.loop(1, DEVICES)
        def _(j):
            send(r, (j * 11) % DEVICES)

    filter_round(1)
    send_round(1)

    for get in gets[2:5]:
        get.wait()
    local = time_in[...] - me * TCH
    quarter = TCH // 4
    within = local % quarter
    code = (local // quarter) * NTEMP + tmpl_in[...]
    size = amp_in[...].astype(jnp.float32)

    @pl.loop(0, quarter // 64)
    def _(i):
        row = lax.broadcasted_iota(jnp.int32, (64, NSP), 0) + i * 64
        hot[pl.ds(pl.multiple_of(i * 64, 64), 64), :] = jnp.where(row == within, 1.0, 0.0).astype(jnp.bfloat16)

    @pl.loop(0, 4)
    def _(q):
        @pl.loop(0, NTEMP // 64)
        def _(i):
            row = lax.broadcasted_iota(jnp.int32, (64, NSP), 0) + (i * 64 + q * NTEMP)
            picked[pl.ds(pl.multiple_of(i * 64, 64), 64), :] = jnp.where(row == code, size, 0.0).astype(jnp.bfloat16)

        @pl.loop(0, quarter // 256)
        def _(m):
            total = lax.dot_general(
                hot[pl.ds(pl.multiple_of(m * 256, 256), 256), :], picked[...],
                (((1,), (1,)), ((), ())), preferred_element_type=jnp.float32,
            )
            at = pl.multiple_of(HW + q * quarter + m * 256, 32)
            events[pl.ds(at, 256), :] = total.astype(jnp.bfloat16)

    def to_next():
        return pltpu.make_async_remote_copy(
            src_ref=events.at[pl.ds(TCH, HW), :],
            dst_ref=events.at[pl.ds(0, HW), :],
            send_sem=halo_send.at[0],
            recv_sem=halo_recv.at[0],
            device_id={"tm": (me + 1) % DEVICES},
            device_id_type=MESH,
        )

    def to_prev():
        return pltpu.make_async_remote_copy(
            src_ref=events.at[pl.ds(HW, HW), :],
            dst_ref=events.at[pl.ds(TCH + HW, HW), :],
            send_sem=halo_send.at[1],
            recv_sem=halo_recv.at[1],
            device_id={"tm": (me + DEVICES - 1) % DEVICES},
            device_id_type=MESH,
        )

    none = jnp.zeros((HW, NTEMP), jnp.bfloat16)

    @pl.when(me == 0)
    def _():
        events[0:HW, :] = none

    @pl.when(me == DEVICES - 1)
    def _():
        events[TCH + HW : TCH + 2 * HW, :] = none

    @pl.when(me < DEVICES - 1)
    def _():
        to_next().start()

    @pl.when(me > 0)
    def _():
        to_prev().start()

    filter_round(2)
    send_round(2)
    filter_round(3)
    send_round(3)

    gets[5].wait()

    def load_rows(at, count):
        part = events[pl.ds(at, count), :]
        for r in range(RANK):
            value = jnp.dot(part, smat[r], preferred_element_type=jnp.float32)
            loads[pl.ds(at, count), r * PCH : (r + 1) * PCH] = value.astype(jnp.bfloat16)

    @pl.loop(0, TCH // 256)
    def _(i):
        load_rows(pl.multiple_of(HW + i * 256, 32), 256)

    for r in range(RANK):
        spread = jnp.broadcast_to(-rows[r : r + 1, :], (256, 256))
        ring = pltpu.roll(spread, 192, 1, stride=1, stride_axis=0)
        bands[r] = ring.T.astype(jnp.bfloat16)

    @pl.when(me > 0)
    def _():
        to_next().wait_recv()

    @pl.when(me < DEVICES - 1)
    def _():
        to_prev().wait_recv()

    load_rows(0, HW)
    load_rows(TCH + HW, HW)

    def spill(at):
        total = jnp.zeros((STEP, PCH), jnp.float32)
        for r in range(RANK):
            total += jnp.dot(
                bands[r, :STEP, :], loads[pl.ds(at, 256), r * PCH : (r + 1) * PCH],
                preferred_element_type=jnp.float32,
            )
        out[pl.ds(at, STEP), :] = total

    @pl.loop(0, TCH // STEP)
    def _(i):
        spill(pl.multiple_of(i * STEP, 64))

    spill(TCH - STEP)

    gets[6].wait()

    @pl.loop(0, ROUNDS)
    def _(r):
        several = pl.ds(0, DEVICES - 1)
        pltpu.make_async_copy(outbox.at[r, several], inbox.at[r, several], recv_sem.at[r]).wait()
        turned[...] = inbox[r].reshape(DEVICES * ROWS, LANE).astype(jnp.float32)
        for b in range(PER):
            block = turned[pl.ds(b, PCH, stride=PER), :].T.astype(jnp.bfloat16)
            value = jnp.dot(block, wmat[...], preferred_element_type=jnp.float32)
            at = pl.ds(pl.multiple_of((r * PER + b) * LANE, LANE), LANE)
            out[at, :] = out[at, :] + value

    for r in range(ROUNDS):
        several = pl.ds(0, DEVICES - 1)
        pltpu.make_async_copy(outbox.at[r, several], inbox.at[r, several], send_sem.at[r]).wait()

    @pl.when(me < DEVICES - 1)
    def _():
        to_next().wait_send()

    @pl.when(me > 0)
    def _():
        to_prev().wait_send()


def on_device(raw, whitening, taps, temporal, spatial, spike_time, spike_template, spike_amp):
    bf16, f32 = jnp.bfloat16, jnp.float32
    whole = pl.BlockSpec(memory_space=pltpu.VMEM)
    far = pl.BlockSpec(memory_space=pltpu.HBM)
    samples = TCH * DEVICES
    arrays = (
        raw.reshape(CH, samples // LANE, LANE),
        whitening[0],
        taps[None],
        temporal,
        spatial[0],
        spike_time,
        spike_template,
        spike_amp,
    )
    cleaned = pl.pallas_call(
        kernel,
        out_shape=pltpu.VMEM((TCH, PCH), f32),
        in_specs=[far] * 8,
        out_specs=whole,
        scratch_shapes=[
            pltpu.VMEM((CH, samples // LANE + 16, LANE), f32),
            pltpu.VMEM((GROUP * ROWS, 256), bf16),
            pltpu.VMEM((ROUNDS, DEVICES, ROWS, LANE), bf16),
            pltpu.VMEM((ROUNDS, DEVICES, ROWS, LANE), bf16),
            pltpu.VMEM((TCH // 4, NSP), bf16),
            pltpu.VMEM((NTEMP, NSP), bf16),
            pltpu.VMEM((TCH + 2 * HW, NTEMP), bf16),
            pltpu.VMEM((TCH + 2 * HW, RANK * PCH), bf16),
            pltpu.VMEM((DEVICES * ROWS, LANE), f32),
            pltpu.VMEM((256, 256), bf16),
            pltpu.VMEM((RANK, 256, 256), bf16),
            pltpu.VMEM((PCH, PCH), bf16),
            pltpu.VMEM((RANK, NTEMP, PCH), bf16),
            pltpu.VMEM((1, NTAP), f32),
            pltpu.VMEM((RANK, NTAP), bf16),
            pltpu.VMEM((1, NSP), jnp.int32),
            pltpu.VMEM((1, NSP), jnp.int32),
            pltpu.VMEM((1, NSP), bf16),
            pltpu.VMEM((8, 256), f32),
            pltpu.SemaphoreType.DMA,
            pltpu.SemaphoreType.DMA((7,)),
            pltpu.SemaphoreType.DMA((ROUNDS,)),
            pltpu.SemaphoreType.DMA((ROUNDS,)),
            pltpu.SemaphoreType.DMA((2,)),
            pltpu.SemaphoreType.DMA((2,)),
            pltpu.SemaphoreType.REGULAR,
            pltpu.SemaphoreType.REGULAR,
        ],
        compiler_params=pltpu.CompilerParams(
            collective_id=0, has_side_effects=True, vmem_limit_bytes=46 * 2**20
        ),
    )(*(pltpu.with_memory_space_constraint(array, pltpu.HBM) for array in arrays))
    return cleaned[None]


def solution(mesh):
    return jax.shard_map(
        on_device,
        mesh=mesh,
        in_specs=(
            P("probe", "tm", None),
            P("probe", None, None),
            P(),
            P(),
            P("probe", None, None, None),
            P("probe", "tm"),
            P("probe", "tm"),
            P("probe", "tm"),
        ),
        out_specs=P("probe", "tm", None),
        check_vma=False,
    )
```

```python
import jax
import jax.numpy as jnp
from jax import lax
from jax.experimental import pallas as pl
from jax.experimental.pallas import tpu as pltpu
from jax.sharding import PartitionSpec as P

MESH = pl.DeviceIdType.MESH
DEVICES = 32
CH = 12
PCH = 384
NTEMP = 256
RANK = 3
NTAP = 65
TCH = 4096
NSP = 2048
LANE = 128
BLOCKS = TCH // LANE
ROUNDS = 4
PER = BLOCKS // ROUNDS
ROWS = CH * PER
HW = 32
GROUP = 8
STEP = 192
MARGIN = 16


def hops(k):
    return k % 2 + min(k // 2 % 4, 4 - k // 2 % 4) + min(k // 8, 4 - k // 8)


ORDER = sorted(range(DEVICES), key=lambda k: -hops(k))


def partner(me, k):
    x, y, z = me // 16, (me // 4) % 4, me % 4
    x = (x + k % 2) % 2
    y = (y + (k // 2) % 4) % 4
    z = (z + k // 8) % 4
    return x * 16 + y * 4 + z


def whiten(turned, b, wmat):
    block = turned[pl.ds(b, PCH, stride=PER), :].T.astype(jnp.bfloat16)
    return jnp.dot(block, wmat, preferred_element_type=jnp.float32)


def kernel(
    raw, white, taps, temporal, spatial, time, tmpl, amp, out, late,
    wide, outbox, inbox, hot, picked, events, loads, turned, band, bands, wmat, smat,
    taps_in, temporal_in, time_in, tmpl_in, amp_in, rows, lines,
    raw_sem, mat_sem, send_sem, recv_sem, halo_send, halo_recv,
):
    me = lax.axis_index("tm")

    barrier = pltpu.get_barrier_semaphore()

    for k in ORDER[:-1]:
        pl.semaphore_signal(barrier, inc=1, device_id={"tm": partner(me, k)}, device_id_type=MESH)

    small = ((taps, taps_in), (temporal, temporal_in), (time, time_in), (tmpl, tmpl_in), (amp, amp_in))
    gets = [
        pltpu.make_async_copy(there, here, mat_sem.at[i])
        for i, (there, here) in enumerate(small + ((spatial, smat), (white, wmat)))
    ]
    for get in gets[:2]:
        get.start()

    def fetch(i):
        to = partner(me, ORDER[i])
        start = 32 * to - 8 * ((to + 31) // 32) - 8 * ((to + 1) // 32)
        return pltpu.make_async_copy(
            raw.at[:, pl.ds(pl.multiple_of(start, 8), 48), :],
            wide.at[i, :, pl.ds(pl.multiple_of(start - 32 * to + MARGIN, 8), 48), :],
            raw_sem.at[i],
        )

    edge = jnp.zeros((CH, 8, LANE), jnp.float32)

    for i in range(DEVICES):
        fetch(i).start()
        to = partner(me, ORDER[i])

        @pl.when(to == 0)
        def _(i=i):
            wide[i, :, MARGIN - 8 : MARGIN, :] = edge

        @pl.when(to == DEVICES - 1)
        def _(i=i):
            wide[i, :, MARGIN + BLOCKS : MARGIN + BLOCKS + 8, :] = edge

    for get in gets[2:]:
        get.start()

    rows[...] = jnp.zeros((8, 256), jnp.float32)
    gets[0].wait()
    rows[RANK : RANK + 1, 0:NTAP] = taps_in[...]
    gets[1].wait()
    rows[0:RANK, 0:NTAP] = temporal_in[...].astype(jnp.float32)

    fine = rows[RANK : RANK + 1, :]
    coarse = fine.astype(jnp.bfloat16).astype(jnp.float32)
    for i, part in enumerate((coarse, fine - coarse)):
        spread = jnp.broadcast_to(part, (LANE, 256))
        ring = pltpu.roll(spread, 224, 1, stride=1, stride_axis=0)
        band[:, i * LANE : (i + 1) * LANE] = ring.T.astype(jnp.bfloat16)

    def send(r, i):
        last = r == ROUNDS - 1
        pltpu.make_async_remote_copy(
            src_ref=outbox.at[r, i],
            dst_ref=late.at[me] if last else inbox.at[r, me],
            send_sem=send_sem.at[r],
            recv_sem=recv_sem.at[r],
            device_id={"tm": partner(me, ORDER[i])},
            device_id_type=MESH,
        ).start()

    def filter_group(r, g):
        slots, first = pl.ds(g * GROUP, GROUP), MARGIN + r * PER
        here = wide[slots, :, first : first + PER, :].reshape(GROUP * ROWS, LANE)
        behind = wide[slots, :, first - 1 : first - 1 + PER, :].reshape(GROUP * ROWS, LANE)
        ahead = wide[slots, :, first + 1 : first + 1 + PER, :].reshape(GROUP * ROWS, LANE)
        lane = lax.broadcasted_iota(jnp.int32, here.shape, 1)
        beside = jnp.where(lane < 64, ahead, behind)
        both = jnp.dot(
            jnp.concatenate([here.astype(jnp.bfloat16), beside.astype(jnp.bfloat16)], axis=1),
            band[...], preferred_element_type=jnp.float32,
        )
        done = (both[:, :LANE] + both[:, LANE:]).astype(jnp.bfloat16)
        outbox[r, slots] = done.reshape(GROUP, ROWS, LANE)

    def filter_and_send(r):
        @pl.loop(0, DEVICES // GROUP)
        def _(g):
            filter_group(r, g)

        for i in range(DEVICES - 1):
            send(r, i)
        (late if r == ROUNDS - 1 else inbox.at[r])[me] = outbox[r, DEVICES - 1]

    for g in range(DEVICES // GROUP):
        for j in range(GROUP):
            fetch(g * GROUP + j).wait()
        filter_group(0, g)
        if g == 0:
            pl.semaphore_wait(barrier, DEVICES - 1)
        for j in range(GROUP):
            if g * GROUP + j < DEVICES - 1:
                send(0, g * GROUP + j)
    inbox[0, me] = outbox[0, DEVICES - 1]
    filter_and_send(1)

    for get in gets[2:5]:
        get.wait()
    local = time_in[...] - me * TCH
    quarter = TCH // 4
    within = local % quarter
    code = (local // quarter) * NTEMP + tmpl_in[...]
    size = amp_in[...].astype(jnp.float32)
    for j in range(NSP // LANE):
        lines[0, j : j + 1, :] = code[:, j * LANE : (j + 1) * LANE].astype(jnp.float32)
        lines[1, j : j + 1, :] = size[:, j * LANE : (j + 1) * LANE]
    codes, sizes = lines[0].T, lines[1].T

    @pl.loop(0, quarter // 64)
    def _(i):
        row = lax.broadcasted_iota(jnp.int32, (64, NSP), 0) + i * 64
        hot[pl.ds(pl.multiple_of(i * 64, 64), 64), :] = jnp.where(row == within, 1.0, 0.0).astype(jnp.bfloat16)

    for q in range(4):
        column = (lax.broadcasted_iota(jnp.int32, (LANE, NTEMP), 1) + q * NTEMP).astype(jnp.float32)
        for j in range(NSP // LANE):
            mine = jnp.where(column == codes[:, j : j + 1], sizes[:, j : j + 1], 0.0)
            picked[j * LANE : (j + 1) * LANE, :] = mine.astype(jnp.bfloat16)

        @pl.loop(0, quarter // 256)
        def _(m):
            total = jnp.dot(
                hot[pl.ds(pl.multiple_of(m * 256, 256), 256), :], picked[...],
                preferred_element_type=jnp.float32,
            )
            at = pl.multiple_of(HW + q * quarter + m * 256, 32)
            events[pl.ds(at, 256), :] = total.astype(jnp.bfloat16)

    def to_next():
        return pltpu.make_async_remote_copy(
            src_ref=events.at[pl.ds(TCH, HW), :],
            dst_ref=events.at[pl.ds(0, HW), :],
            send_sem=halo_send.at[0],
            recv_sem=halo_recv.at[0],
            device_id={"tm": (me + 1) % DEVICES},
            device_id_type=MESH,
        )

    def to_prev():
        return pltpu.make_async_remote_copy(
            src_ref=events.at[pl.ds(HW, HW), :],
            dst_ref=events.at[pl.ds(TCH + HW, HW), :],
            send_sem=halo_send.at[1],
            recv_sem=halo_recv.at[1],
            device_id={"tm": (me + DEVICES - 1) % DEVICES},
            device_id_type=MESH,
        )

    none = jnp.zeros((HW, NTEMP), jnp.bfloat16)

    @pl.when(me == 0)
    def _():
        events[0:HW, :] = none

    @pl.when(me == DEVICES - 1)
    def _():
        events[TCH + HW : TCH + 2 * HW, :] = none

    @pl.when(me < DEVICES - 1)
    def _():
        to_next().start()

    @pl.when(me > 0)
    def _():
        to_prev().start()

    filter_and_send(2)
    filter_and_send(3)

    gets[5].wait()

    def load_rows(at, count):
        part = events[pl.ds(at, count), :]
        for r in range(RANK):
            value = jnp.dot(part, smat[r], preferred_element_type=jnp.float32)
            loads[pl.ds(at, count), r * PCH : (r + 1) * PCH] = value.astype(jnp.bfloat16)

    @pl.loop(0, TCH // 256)
    def _(i):
        load_rows(pl.multiple_of(HW + i * 256, 32), 256)

    for r in range(RANK):
        spread = jnp.broadcast_to(-rows[r : r + 1, :], (256, 256))
        ring = pltpu.roll(spread, 192, 1, stride=1, stride_axis=0)
        bands[:, r * 256 : (r + 1) * 256] = ring.T[:STEP].astype(jnp.bfloat16)

    @pl.when(me > 0)
    def _():
        to_next().wait_recv()

    @pl.when(me < DEVICES - 1)
    def _():
        to_prev().wait_recv()

    load_rows(0, HW)
    load_rows(TCH + HW, HW)

    def spill(at):
        part = jnp.concatenate([loads[pl.ds(at, 256), r * PCH : (r + 1) * PCH] for r in range(RANK)], axis=0)
        out[pl.ds(at, STEP), :] = jnp.dot(bands[...], part, preferred_element_type=jnp.float32)

    @pl.loop(0, TCH // STEP // 3)
    def _(i):
        for j in range(3):
            spill(pl.multiple_of(i * (3 * STEP) + j * STEP, 64))

    spill(TCH - STEP)

    gets[6].wait()
    several = pl.ds(0, DEVICES - 1)

    @pl.loop(0, ROUNDS - 1)
    def _(r):
        pltpu.make_async_copy(outbox.at[r, several], inbox.at[r, several], recv_sem.at[r]).wait()
        turned[...] = inbox[r].reshape(DEVICES * ROWS, LANE).astype(jnp.float32)
        for b in range(PER):
            at = pl.ds(pl.multiple_of((r * PER + b) * LANE, LANE), LANE)
            out[at, :] = out[at, :] + whiten(turned, b, wmat[...])

    r = ROUNDS - 1
    pltpu.make_async_copy(outbox.at[r, several], late.at[several], recv_sem.at[r]).wait()
    for r in range(ROUNDS):
        pltpu.make_async_copy(outbox.at[r, several], outbox.at[r, several], send_sem.at[r]).wait()

    @pl.when(me < DEVICES - 1)
    def _():
        to_next().wait_send()

    @pl.when(me > 0)
    def _():
        to_prev().wait_send()


def finish(partial, late, white, out, turned, wmat, last, mat_sem, out_sem):
    get = pltpu.make_async_copy(white, wmat, mat_sem)
    get.start()
    done = (ROUNDS - 1) * PER * LANE
    puts = []
    for i in range(ROUNDS - 1):
        at = pl.ds(i * PER * LANE, PER * LANE)
        puts.append(pltpu.make_async_copy(partial.at[at, :], out.at[at, :], out_sem.at[i]))
    for put in puts:
        put.start()
    turned[...] = late[...].reshape(DEVICES * ROWS, LANE).astype(jnp.float32)
    get.wait()
    for b in range(PER):
        rows = pl.ds(b * LANE, LANE)
        last[rows, :] = partial[done + b * LANE : done + (b + 1) * LANE, :] + whiten(turned, b, wmat[...])
        if b % 4 == 3:
            rows = pl.ds((b - 3) * LANE, 4 * LANE)
            put = pltpu.make_async_copy(
                last.at[rows, :], out.at[pl.ds(done + (b - 3) * LANE, 4 * LANE), :], out_sem.at[ROUNDS - 1 + b // 4]
            )
            put.start()
            puts.append(put)
    for put in puts:
        put.wait()


def on_device(raw, whitening, taps, temporal, spatial, spike_time, spike_template, spike_amp):
    bf16, f32 = jnp.bfloat16, jnp.float32
    whole = pl.BlockSpec(memory_space=pltpu.VMEM)
    far = pl.BlockSpec(memory_space=pltpu.HBM)
    samples = TCH * DEVICES
    arrays = tuple(pltpu.with_memory_space_constraint(array, pltpu.HBM) for array in (
        raw.reshape(CH, samples // LANE, LANE),
        whitening[0],
        taps[None],
        temporal,
        spatial[0],
        spike_time,
        spike_template,
        spike_amp,
    ))
    partial, late = pl.pallas_call(
        kernel,
        out_shape=(pltpu.VMEM((TCH, PCH), f32), pltpu.VMEM((DEVICES, ROWS, LANE), bf16)),
        in_specs=[far] * 8,
        out_specs=(whole, whole),
        scratch_shapes=[
            pltpu.VMEM((DEVICES, CH, 64, LANE), f32),
            pltpu.VMEM((ROUNDS, DEVICES, ROWS, LANE), bf16),
            pltpu.VMEM((ROUNDS - 1, DEVICES, ROWS, LANE), bf16),
            pltpu.VMEM((TCH // 4, NSP), bf16),
            pltpu.VMEM((NSP, NTEMP), bf16),
            pltpu.VMEM((TCH + 2 * HW, NTEMP), bf16),
            pltpu.VMEM((TCH + 2 * HW, RANK * PCH), bf16),
            pltpu.VMEM((DEVICES * ROWS, LANE), f32),
            pltpu.VMEM((256, 256), bf16),
            pltpu.VMEM((STEP, RANK * 256), bf16),
            pltpu.VMEM((PCH, PCH), bf16),
            pltpu.VMEM((RANK, NTEMP, PCH), bf16),
            pltpu.VMEM((1, NTAP), f32),
            pltpu.VMEM((RANK, NTAP), bf16),
            pltpu.VMEM((1, NSP), jnp.int32),
            pltpu.VMEM((1, NSP), jnp.int32),
            pltpu.VMEM((1, NSP), bf16),
            pltpu.VMEM((8, 256), f32),
            pltpu.VMEM((2, NSP // LANE, LANE), f32),
            pltpu.SemaphoreType.DMA((DEVICES,)),
            pltpu.SemaphoreType.DMA((7,)),
            pltpu.SemaphoreType.DMA((ROUNDS,)),
            pltpu.SemaphoreType.DMA((ROUNDS,)),
            pltpu.SemaphoreType.DMA((2,)),
            pltpu.SemaphoreType.DMA((2,)),
        ],
        compiler_params=pltpu.CompilerParams(
            collective_id=0, has_side_effects=True, vmem_limit_bytes=50 * 2**20
        ),
    )(*arrays)
    cleaned = pl.pallas_call(
        finish,
        out_shape=jax.ShapeDtypeStruct((TCH, PCH), f32),
        in_specs=[whole, whole, far],
        out_specs=far,
        scratch_shapes=[
            pltpu.VMEM((DEVICES * ROWS, LANE), f32),
            pltpu.VMEM((PCH, PCH), bf16),
            pltpu.VMEM((PER * LANE, PCH), f32),
            pltpu.SemaphoreType.DMA,
            pltpu.SemaphoreType.DMA((ROUNDS + 1,)),
        ],
        compiler_params=pltpu.CompilerParams(vmem_limit_bytes=16 * 2**20),
    )(
        pltpu.with_memory_space_constraint(partial, pltpu.VMEM),
        pltpu.with_memory_space_constraint(late, pltpu.VMEM),
        arrays[1],
    )
    return cleaned[None]


def solution(mesh):
    return jax.shard_map(
        on_device,
        mesh=mesh,
        in_specs=(
            P("probe", "tm", None),
            P("probe", None, None),
            P(),
            P(),
            P("probe", None, None, None),
            P("probe", "tm"),
            P("probe", "tm"),
            P("probe", "tm"),
        ),
        out_specs=P("probe", "tm", None),
        check_vma=False,
    )
```

```python
import jax
import jax.numpy as jnp
from jax import lax
from jax.experimental import pallas as pl
from jax.experimental.pallas import tpu as pltpu
from jax.sharding import PartitionSpec as P

MESH = pl.DeviceIdType.MESH
DEVICES = 32
CH = 12
PCH = 384
NTEMP = 256
RANK = 3
NTAP = 65
TCH = 4096
NSP = 2048
LANE = 128
BLOCKS = TCH // LANE
ROUNDS = 4
PER = BLOCKS // ROUNDS
ROWS = CH * PER
HW = 32
GROUP = 8
FIRST = 8
STEP = 192
MARGIN = 16


def hops(k):
    return k % 2 + min(k // 2 % 4, 4 - k // 2 % 4) + min(k // 8, 4 - k // 8)


ORDER = [(i * 11) % DEVICES for i in range(1, DEVICES + 1)]


def partner(me, k):
    x, y, z = me // 16, (me // 4) % 4, me % 4
    x = (x + k % 2) % 2
    y = (y + (k // 2) % 4) % 4
    z = (z + k // 8) % 4
    return x * 16 + y * 4 + z


def whiten(turned, b, wmat):
    block = turned[pl.ds(b, PCH, stride=PER), :].T.astype(jnp.bfloat16)
    return jnp.dot(block, wmat, preferred_element_type=jnp.float32)


def kernel(
    raw, white, taps, temporal, spatial, time, tmpl, amp, out, late,
    wide, outbox, inbox, hot, picked, events, loads, turned, band, bands, wmat, smat,
    taps_in, temporal_in, time_in, tmpl_in, amp_in, rows, lines,
    raw_sem, mat_sem, send_sem, recv_sem, halo_send, halo_recv,
):
    me = lax.axis_index("tm")

    barrier = pltpu.get_barrier_semaphore()

    for k in ORDER[:-1]:
        pl.semaphore_signal(barrier, inc=1, device_id={"tm": partner(me, k)}, device_id_type=MESH)

    small = ((taps, taps_in), (temporal, temporal_in), (time, time_in), (tmpl, tmpl_in), (amp, amp_in))
    gets = [
        pltpu.make_async_copy(there, here, mat_sem.at[i])
        for i, (there, here) in enumerate(small + ((spatial, smat), (white, wmat)))
    ]
    for get in gets[:2]:
        get.start()

    def fetch(i):
        to = partner(me, ORDER[i])
        start = 32 * to - 8 * ((to + 31) // 32) - 8 * ((to + 1) // 32)
        return pltpu.make_async_copy(
            raw.at[:, pl.ds(pl.multiple_of(start, 8), 48), :],
            wide.at[i, :, pl.ds(pl.multiple_of(start - 32 * to + MARGIN, 8), 48), :],
            raw_sem.at[i],
        )

    edge = jnp.zeros((CH, 8, LANE), jnp.float32)

    for i in range(DEVICES):
        fetch(i).start()
        to = partner(me, ORDER[i])

        @pl.when(to == 0)
        def _(i=i):
            wide[i, :, MARGIN - 8 : MARGIN, :] = edge

        @pl.when(to == DEVICES - 1)
        def _(i=i):
            wide[i, :, MARGIN + BLOCKS : MARGIN + BLOCKS + 8, :] = edge

    for get in gets[2:]:
        get.start()

    rows[...] = jnp.zeros((8, 256), jnp.float32)
    gets[0].wait()
    rows[RANK : RANK + 1, 0:NTAP] = taps_in[...]
    gets[1].wait()
    rows[0:RANK, 0:NTAP] = temporal_in[...].astype(jnp.float32)

    fine = rows[RANK : RANK + 1, :]
    coarse = fine.astype(jnp.bfloat16).astype(jnp.float32)
    for i, part in enumerate((coarse, fine - coarse)):
        spread = jnp.broadcast_to(part, (LANE, 256))
        ring = pltpu.roll(spread, 224, 1, stride=1, stride_axis=0)
        band[:, i * LANE : (i + 1) * LANE] = ring.T.astype(jnp.bfloat16)

    def send(r, i):
        last = r == ROUNDS - 1
        pltpu.make_async_remote_copy(
            src_ref=outbox.at[r, i],
            dst_ref=late.at[me] if last else inbox.at[r, me],
            send_sem=send_sem.at[r],
            recv_sem=recv_sem.at[r],
            device_id={"tm": partner(me, ORDER[i])},
            device_id_type=MESH,
        ).start()

    def filter_group(r, at, count):
        slots, first = pl.ds(at, count), MARGIN + r * PER
        here = wide[slots, :, first : first + PER, :].reshape(count * ROWS, LANE)
        behind = wide[slots, :, first - 1 : first - 1 + PER, :].reshape(count * ROWS, LANE)
        ahead = wide[slots, :, first + 1 : first + 1 + PER, :].reshape(count * ROWS, LANE)
        lane = lax.broadcasted_iota(jnp.int32, here.shape, 1)
        beside = jnp.where(lane < 64, ahead, behind)
        both = jnp.dot(
            jnp.concatenate([here.astype(jnp.bfloat16), beside.astype(jnp.bfloat16)], axis=1),
            band[...], preferred_element_type=jnp.float32,
        )
        done = (both[:, :LANE] + both[:, LANE:]).astype(jnp.bfloat16)
        outbox[r, slots] = done.reshape(count, ROWS, LANE)

    def filter_and_send(r):
        @pl.loop(0, DEVICES // GROUP)
        def _(g):
            filter_group(r, g * GROUP, GROUP)

        for i in range(DEVICES - 1):
            send(r, i)
        (late if r == ROUNDS - 1 else inbox.at[r])[me] = outbox[r, DEVICES - 1]

    for i in range(0, DEVICES, FIRST):
        for j in range(i, i + FIRST):
            fetch(j).wait()
        filter_group(0, i, FIRST)
        if i == 0:
            pl.semaphore_wait(barrier, DEVICES - 1)
        for j in range(i, min(i + FIRST, DEVICES - 1)):
            send(0, j)
    inbox[0, me] = outbox[0, DEVICES - 1]
    filter_and_send(1)

    for get in gets[2:5]:
        get.wait()
    local = time_in[...] - me * TCH
    quarter = TCH // 4
    within = local % quarter
    code = (local // quarter) * NTEMP + tmpl_in[...]
    size = amp_in[...].astype(jnp.float32)
    for j in range(NSP // LANE):
        lines[0, j : j + 1, :] = code[:, j * LANE : (j + 1) * LANE].astype(jnp.float32)
        lines[1, j : j + 1, :] = size[:, j * LANE : (j + 1) * LANE]
    codes, sizes = lines[0].T, lines[1].T

    @pl.loop(0, quarter // 64)
    def _(i):
        row = lax.broadcasted_iota(jnp.int32, (64, NSP), 0) + i * 64
        hot[pl.ds(pl.multiple_of(i * 64, 64), 64), :] = jnp.where(row == within, 1.0, 0.0).astype(jnp.bfloat16)

    for q in range(4):
        column = (lax.broadcasted_iota(jnp.int32, (LANE, NTEMP), 1) + q * NTEMP).astype(jnp.float32)
        for j in range(NSP // LANE):
            mine = jnp.where(column == codes[:, j : j + 1], sizes[:, j : j + 1], 0.0)
            picked[j * LANE : (j + 1) * LANE, :] = mine.astype(jnp.bfloat16)

        @pl.loop(0, quarter // 256)
        def _(m):
            total = jnp.dot(
                hot[pl.ds(pl.multiple_of(m * 256, 256), 256), :], picked[...],
                preferred_element_type=jnp.float32,
            )
            at = pl.multiple_of(HW + q * quarter + m * 256, 32)
            events[pl.ds(at, 256), :] = total.astype(jnp.bfloat16)

    def to_next():
        return pltpu.make_async_remote_copy(
            src_ref=events.at[pl.ds(TCH, HW), :],
            dst_ref=events.at[pl.ds(0, HW), :],
            send_sem=halo_send.at[0],
            recv_sem=halo_recv.at[0],
            device_id={"tm": (me + 1) % DEVICES},
            device_id_type=MESH,
        )

    def to_prev():
        return pltpu.make_async_remote_copy(
            src_ref=events.at[pl.ds(HW, HW), :],
            dst_ref=events.at[pl.ds(TCH + HW, HW), :],
            send_sem=halo_send.at[1],
            recv_sem=halo_recv.at[1],
            device_id={"tm": (me + DEVICES - 1) % DEVICES},
            device_id_type=MESH,
        )

    none = jnp.zeros((HW, NTEMP), jnp.bfloat16)

    @pl.when(me == 0)
    def _():
        events[0:HW, :] = none

    @pl.when(me == DEVICES - 1)
    def _():
        events[TCH + HW : TCH + 2 * HW, :] = none

    @pl.when(me < DEVICES - 1)
    def _():
        to_next().start()

    @pl.when(me > 0)
    def _():
        to_prev().start()

    filter_and_send(2)
    filter_and_send(3)

    gets[5].wait()

    def load_rows(at, count):
        part = events[pl.ds(at, count), :]
        for r in range(RANK):
            value = jnp.dot(part, smat[r], preferred_element_type=jnp.float32)
            loads[pl.ds(at, count), r * PCH : (r + 1) * PCH] = value.astype(jnp.bfloat16)

    @pl.loop(0, TCH // 256)
    def _(i):
        load_rows(pl.multiple_of(HW + i * 256, 32), 256)

    for r in range(RANK):
        spread = jnp.broadcast_to(-rows[r : r + 1, :], (256, 256))
        ring = pltpu.roll(spread, 192, 1, stride=1, stride_axis=0)
        bands[:, r * 256 : (r + 1) * 256] = ring.T[:STEP].astype(jnp.bfloat16)

    @pl.when(me > 0)
    def _():
        to_next().wait_recv()

    @pl.when(me < DEVICES - 1)
    def _():
        to_prev().wait_recv()

    load_rows(0, HW)
    load_rows(TCH + HW, HW)

    def spill(at):
        part = jnp.concatenate([loads[pl.ds(at, 256), r * PCH : (r + 1) * PCH] for r in range(RANK)], axis=0)
        out[pl.ds(at, STEP), :] = jnp.dot(bands[...], part, preferred_element_type=jnp.float32)

    @pl.loop(0, TCH // STEP // 3)
    def _(i):
        for j in range(3):
            spill(pl.multiple_of(i * (3 * STEP) + j * STEP, 64))

    spill(TCH - STEP)

    gets[6].wait()
    several = pl.ds(0, DEVICES - 1)

    @pl.loop(0, ROUNDS - 1)
    def _(r):
        pltpu.make_async_copy(outbox.at[r, several], inbox.at[r, several], recv_sem.at[r]).wait()
        turned[...] = inbox[r].reshape(DEVICES * ROWS, LANE).astype(jnp.float32)
        for b in range(PER):
            at = pl.ds(pl.multiple_of((r * PER + b) * LANE, LANE), LANE)
            out[at, :] = out[at, :] + whiten(turned, b, wmat[...])

    r = ROUNDS - 1
    pltpu.make_async_copy(outbox.at[r, several], late.at[several], recv_sem.at[r]).wait()
    for r in range(ROUNDS):
        pltpu.make_async_copy(outbox.at[r, several], outbox.at[r, several], send_sem.at[r]).wait()

    @pl.when(me < DEVICES - 1)
    def _():
        to_next().wait_send()

    @pl.when(me > 0)
    def _():
        to_prev().wait_send()


def finish(partial, late, white, out, turned, wmat, last, mat_sem, out_sem):
    get = pltpu.make_async_copy(white, wmat, mat_sem)
    get.start()
    done = (ROUNDS - 1) * PER * LANE
    puts = []
    for i in range(ROUNDS - 1):
        at = pl.ds(i * PER * LANE, PER * LANE)
        puts.append(pltpu.make_async_copy(partial.at[at, :], out.at[at, :], out_sem.at[i]))
    for put in puts:
        put.start()
    turned[...] = late[...].reshape(DEVICES * ROWS, LANE).astype(jnp.float32)
    get.wait()
    for b in range(PER):
        rows = pl.ds(b * LANE, LANE)
        last[rows, :] = partial[done + b * LANE : done + (b + 1) * LANE, :] + whiten(turned, b, wmat[...])
        put = pltpu.make_async_copy(
            last.at[rows, :], out.at[pl.ds(done + b * LANE, LANE), :], out_sem.at[ROUNDS - 1 + b]
        )
        put.start()
        puts.append(put)
    for put in puts:
        put.wait()


def on_device(raw, whitening, taps, temporal, spatial, spike_time, spike_template, spike_amp):
    bf16, f32 = jnp.bfloat16, jnp.float32
    whole = pl.BlockSpec(memory_space=pltpu.VMEM)
    far = pl.BlockSpec(memory_space=pltpu.HBM)
    samples = TCH * DEVICES
    arrays = tuple(pltpu.with_memory_space_constraint(array, pltpu.HBM) for array in (
        raw.reshape(CH, samples // LANE, LANE),
        whitening[0],
        taps[None],
        temporal,
        spatial[0],
        spike_time,
        spike_template,
        spike_amp,
    ))
    partial, late = pl.pallas_call(
        kernel,
        out_shape=(pltpu.VMEM((TCH, PCH), f32), pltpu.VMEM((DEVICES, ROWS, LANE), bf16)),
        in_specs=[far] * 8,
        out_specs=(whole, whole),
        scratch_shapes=[
            pltpu.VMEM((DEVICES, CH, 64, LANE), f32),
            pltpu.VMEM((ROUNDS, DEVICES, ROWS, LANE), bf16),
            pltpu.VMEM((ROUNDS - 1, DEVICES, ROWS, LANE), bf16),
            pltpu.VMEM((TCH // 4, NSP), bf16),
            pltpu.VMEM((NSP, NTEMP), bf16),
            pltpu.VMEM((TCH + 2 * HW, NTEMP), bf16),
            pltpu.VMEM((TCH + 2 * HW, RANK * PCH), bf16),
            pltpu.VMEM((DEVICES * ROWS, LANE), f32),
            pltpu.VMEM((256, 256), bf16),
            pltpu.VMEM((STEP, RANK * 256), bf16),
            pltpu.VMEM((PCH, PCH), bf16),
            pltpu.VMEM((RANK, NTEMP, PCH), bf16),
            pltpu.VMEM((1, NTAP), f32),
            pltpu.VMEM((RANK, NTAP), bf16),
            pltpu.VMEM((1, NSP), jnp.int32),
            pltpu.VMEM((1, NSP), jnp.int32),
            pltpu.VMEM((1, NSP), bf16),
            pltpu.VMEM((8, 256), f32),
            pltpu.VMEM((2, NSP // LANE, LANE), f32),
            pltpu.SemaphoreType.DMA((DEVICES,)),
            pltpu.SemaphoreType.DMA((7,)),
            pltpu.SemaphoreType.DMA((ROUNDS,)),
            pltpu.SemaphoreType.DMA((ROUNDS,)),
            pltpu.SemaphoreType.DMA((2,)),
            pltpu.SemaphoreType.DMA((2,)),
        ],
        compiler_params=pltpu.CompilerParams(
            collective_id=0, has_side_effects=True, vmem_limit_bytes=50 * 2**20
        ),
    )(*arrays)
    cleaned = pl.pallas_call(
        finish,
        out_shape=jax.ShapeDtypeStruct((TCH, PCH), f32),
        in_specs=[whole, whole, far],
        out_specs=far,
        scratch_shapes=[
            pltpu.VMEM((DEVICES * ROWS, LANE), f32),
            pltpu.VMEM((PCH, PCH), bf16),
            pltpu.VMEM((PER * LANE, PCH), f32),
            pltpu.SemaphoreType.DMA,
            pltpu.SemaphoreType.DMA((ROUNDS - 1 + PER,)),
        ],
        compiler_params=pltpu.CompilerParams(vmem_limit_bytes=16 * 2**20),
    )(
        pltpu.with_memory_space_constraint(partial, pltpu.VMEM),
        pltpu.with_memory_space_constraint(late, pltpu.VMEM),
        arrays[1],
    )
    return cleaned[None]


def solution(mesh):
    return jax.shard_map(
        on_device,
        mesh=mesh,
        in_specs=(
            P("probe", "tm", None),
            P("probe", None, None),
            P(),
            P(),
            P("probe", None, None, None),
            P("probe", "tm"),
            P("probe", "tm"),
            P("probe", "tm"),
        ),
        out_specs=P("probe", "tm", None),
        check_vma=False,
    )
```

```python
import jax
import jax.numpy as jnp
from jax import lax
from jax.experimental import pallas as pl
from jax.experimental.pallas import tpu as pltpu
from jax.sharding import PartitionSpec as P

MESH = pl.DeviceIdType.MESH
DEVICES = 32
CH = 12
PCH = 384
NTEMP = 256
RANK = 3
NTAP = 65
TCH = 4096
NSP = 2048
LANE = 128
BLOCKS = TCH // LANE
ROUNDS = 4
PER = BLOCKS // ROUNDS
ROWS = CH * PER
HW = 32
GROUP = 8
FIRST = 8
STEP = 192
MARGIN = 16


def hops(k):
    return k % 2 + min(k // 2 % 4, 4 - k // 2 % 4) + min(k // 8, 4 - k // 8)


ORDER = [(i * 13) % DEVICES for i in range(1, DEVICES + 1)]


def partner(me, k):
    x, y, z = me // 16, (me // 4) % 4, me % 4
    x = (x + k % 2) % 2
    y = (y + (k // 2) % 4) % 4
    z = (z + k // 8) % 4
    return x * 16 + y * 4 + z


def whiten(turned, b, wmat):
    block = turned[pl.ds(b, PCH, stride=PER), :].T.astype(jnp.bfloat16)
    return jnp.dot(block, wmat, preferred_element_type=jnp.float32)


def kernel(
    raw, white, taps, temporal, spatial, time, tmpl, amp, out, late,
    wide, outbox, inbox, hot, picked, events, loads, turned, band, bands, wmat, smat,
    taps_in, temporal_in, time_in, tmpl_in, amp_in, rows, lines,
    raw_sem, mat_sem, send_sem, recv_sem, halo_send, halo_recv,
):
    me = lax.axis_index("tm")

    barrier = pltpu.get_barrier_semaphore()

    for k in ORDER[:-1]:
        pl.semaphore_signal(barrier, inc=1, device_id={"tm": partner(me, k)}, device_id_type=MESH)

    small = ((taps, taps_in), (temporal, temporal_in), (time, time_in), (tmpl, tmpl_in), (amp, amp_in))
    gets = [
        pltpu.make_async_copy(there, here, mat_sem.at[i])
        for i, (there, here) in enumerate(small + ((spatial, smat), (white, wmat)))
    ]
    for get in gets[:2]:
        get.start()

    def fetch(i):
        to = partner(me, ORDER[i])
        start = 32 * to - 8 * ((to + 31) // 32) - 8 * ((to + 1) // 32)
        return pltpu.make_async_copy(
            raw.at[:, pl.ds(pl.multiple_of(start, 8), 48), :],
            wide.at[i, :, pl.ds(pl.multiple_of(start - 32 * to + MARGIN, 8), 48), :],
            raw_sem.at[i],
        )

    edge = jnp.zeros((CH, 8, LANE), jnp.float32)

    for i in range(DEVICES):
        fetch(i).start()
        to = partner(me, ORDER[i])

        @pl.when(to == 0)
        def _(i=i):
            wide[i, :, MARGIN - 8 : MARGIN, :] = edge

        @pl.when(to == DEVICES - 1)
        def _(i=i):
            wide[i, :, MARGIN + BLOCKS : MARGIN + BLOCKS + 8, :] = edge

    for get in gets[2:]:
        get.start()

    rows[...] = jnp.zeros((8, 256), jnp.float32)
    gets[0].wait()
    rows[RANK : RANK + 1, 0:NTAP] = taps_in[...]
    gets[1].wait()
    rows[0:RANK, 0:NTAP] = temporal_in[...].astype(jnp.float32)

    fine = rows[RANK : RANK + 1, :]
    coarse = fine.astype(jnp.bfloat16).astype(jnp.float32)
    for i, part in enumerate((coarse, fine - coarse)):
        spread = jnp.broadcast_to(part, (LANE, 256))
        ring = pltpu.roll(spread, 224, 1, stride=1, stride_axis=0)
        band[:, i * LANE : (i + 1) * LANE] = ring.T.astype(jnp.bfloat16)

    def send(r, i):
        last = r == ROUNDS - 1
        pltpu.make_async_remote_copy(
            src_ref=outbox.at[r, i],
            dst_ref=late.at[me] if last else inbox.at[r, me],
            send_sem=send_sem.at[r],
            recv_sem=recv_sem.at[r],
            device_id={"tm": partner(me, ORDER[i])},
            device_id_type=MESH,
        ).start()

    def filter_group(r, at, count):
        slots, first = pl.ds(at, count), MARGIN + r * PER
        here = wide[slots, :, first : first + PER, :].reshape(count * ROWS, LANE)
        behind = wide[slots, :, first - 1 : first - 1 + PER, :].reshape(count * ROWS, LANE)
        ahead = wide[slots, :, first + 1 : first + 1 + PER, :].reshape(count * ROWS, LANE)
        lane = lax.broadcasted_iota(jnp.int32, here.shape, 1)
        beside = jnp.where(lane < 64, ahead, behind)
        both = jnp.dot(
            jnp.concatenate([here.astype(jnp.bfloat16), beside.astype(jnp.bfloat16)], axis=1),
            band[...], preferred_element_type=jnp.float32,
        )
        done = (both[:, :LANE] + both[:, LANE:]).astype(jnp.bfloat16)
        outbox[r, slots] = done.reshape(count, ROWS, LANE)

    def filter_and_send(r):
        @pl.loop(0, DEVICES // GROUP)
        def _(g):
            filter_group(r, g * GROUP, GROUP)

        for i in range(DEVICES - 1):
            send(r, i)
        (late if r == ROUNDS - 1 else inbox.at[r])[me] = outbox[r, DEVICES - 1]

    for i in range(0, DEVICES, FIRST):
        for j in range(i, i + FIRST):
            fetch(j).wait()
        filter_group(0, i, FIRST)
        if i == 0:
            pl.semaphore_wait(barrier, DEVICES - 1)
        for j in range(i, min(i + FIRST, DEVICES - 1)):
            send(0, j)
    inbox[0, me] = outbox[0, DEVICES - 1]
    filter_and_send(1)

    for get in gets[2:5]:
        get.wait()
    local = time_in[...] - me * TCH
    quarter = TCH // 4
    within = local % quarter
    code = (local // quarter) * NTEMP + tmpl_in[...]
    size = amp_in[...].astype(jnp.float32)
    for j in range(NSP // LANE):
        lines[0, j : j + 1, :] = code[:, j * LANE : (j + 1) * LANE].astype(jnp.float32)
        lines[1, j : j + 1, :] = size[:, j * LANE : (j + 1) * LANE]
    codes, sizes = lines[0].T, lines[1].T

    @pl.loop(0, quarter // 64)
    def _(i):
        row = lax.broadcasted_iota(jnp.int32, (64, NSP), 0) + i * 64
        hot[pl.ds(pl.multiple_of(i * 64, 64), 64), :] = jnp.where(row == within, 1.0, 0.0).astype(jnp.bfloat16)

    for q in range(4):
        column = (lax.broadcasted_iota(jnp.int32, (LANE, NTEMP), 1) + q * NTEMP).astype(jnp.float32)
        for j in range(NSP // LANE):
            mine = jnp.where(column == codes[:, j : j + 1], sizes[:, j : j + 1], 0.0)
            picked[j * LANE : (j + 1) * LANE, :] = mine.astype(jnp.bfloat16)

        @pl.loop(0, quarter // 256)
        def _(m):
            total = jnp.dot(
                hot[pl.ds(pl.multiple_of(m * 256, 256), 256), :], picked[...],
                preferred_element_type=jnp.float32,
            )
            at = pl.multiple_of(HW + q * quarter + m * 256, 32)
            events[pl.ds(at, 256), :] = total.astype(jnp.bfloat16)

    def to_next():
        return pltpu.make_async_remote_copy(
            src_ref=events.at[pl.ds(TCH, HW), :],
            dst_ref=events.at[pl.ds(0, HW), :],
            send_sem=halo_send.at[0],
            recv_sem=halo_recv.at[0],
            device_id={"tm": (me + 1) % DEVICES},
            device_id_type=MESH,
        )

    def to_prev():
        return pltpu.make_async_remote_copy(
            src_ref=events.at[pl.ds(HW, HW), :],
            dst_ref=events.at[pl.ds(TCH + HW, HW), :],
            send_sem=halo_send.at[1],
            recv_sem=halo_recv.at[1],
            device_id={"tm": (me + DEVICES - 1) % DEVICES},
            device_id_type=MESH,
        )

    none = jnp.zeros((HW, NTEMP), jnp.bfloat16)

    @pl.when(me == 0)
    def _():
        events[0:HW, :] = none

    @pl.when(me == DEVICES - 1)
    def _():
        events[TCH + HW : TCH + 2 * HW, :] = none

    @pl.when(me < DEVICES - 1)
    def _():
        to_next().start()

    @pl.when(me > 0)
    def _():
        to_prev().start()

    filter_and_send(2)
    filter_and_send(3)

    gets[5].wait()

    def load_rows(at, count):
        part = events[pl.ds(at, count), :]
        for r in range(RANK):
            value = jnp.dot(part, smat[r], preferred_element_type=jnp.float32)
            loads[pl.ds(at, count), r * PCH : (r + 1) * PCH] = value.astype(jnp.bfloat16)

    @pl.loop(0, TCH // 256)
    def _(i):
        load_rows(pl.multiple_of(HW + i * 256, 32), 256)

    for r in range(RANK):
        spread = jnp.broadcast_to(-rows[r : r + 1, :], (256, 256))
        ring = pltpu.roll(spread, 192, 1, stride=1, stride_axis=0)
        bands[:, r * 256 : (r + 1) * 256] = ring.T[:STEP].astype(jnp.bfloat16)

    @pl.when(me > 0)
    def _():
        to_next().wait_recv()

    @pl.when(me < DEVICES - 1)
    def _():
        to_prev().wait_recv()

    load_rows(0, HW)
    load_rows(TCH + HW, HW)

    def spill(at):
        part = jnp.concatenate([loads[pl.ds(at, 256), r * PCH : (r + 1) * PCH] for r in range(RANK)], axis=0)
        out[pl.ds(at, STEP), :] = jnp.dot(bands[...], part, preferred_element_type=jnp.float32)

    @pl.loop(0, TCH // STEP // 3)
    def _(i):
        for j in range(3):
            spill(pl.multiple_of(i * (3 * STEP) + j * STEP, 64))

    spill(TCH - STEP)

    gets[6].wait()
    several = pl.ds(0, DEVICES - 1)

    @pl.loop(0, ROUNDS - 1)
    def _(r):
        pltpu.make_async_copy(outbox.at[r, several], inbox.at[r, several], recv_sem.at[r]).wait()
        turned[...] = inbox[r].reshape(DEVICES * ROWS, LANE).astype(jnp.float32)
        for b in range(PER):
            at = pl.ds(pl.multiple_of((r * PER + b) * LANE, LANE), LANE)
            out[at, :] = out[at, :] + whiten(turned, b, wmat[...])

    r = ROUNDS - 1
    pltpu.make_async_copy(outbox.at[r, several], late.at[several], recv_sem.at[r]).wait()
    for r in range(ROUNDS):
        pltpu.make_async_copy(outbox.at[r, several], outbox.at[r, several], send_sem.at[r]).wait()

    @pl.when(me < DEVICES - 1)
    def _():
        to_next().wait_send()

    @pl.when(me > 0)
    def _():
        to_prev().wait_send()


def finish(partial, late, white, out, turned, wmat, last, mat_sem, out_sem):
    get = pltpu.make_async_copy(white, wmat, mat_sem)
    get.start()
    done = (ROUNDS - 1) * PER * LANE
    puts = []
    for i in range(ROUNDS - 1):
        at = pl.ds(i * PER * LANE, PER * LANE)
        puts.append(pltpu.make_async_copy(partial.at[at, :], out.at[at, :], out_sem.at[i]))
    for put in puts:
        put.start()
    turned[...] = late[...].reshape(DEVICES * ROWS, LANE).astype(jnp.float32)
    get.wait()
    for b in range(PER):
        rows = pl.ds(b * LANE, LANE)
        last[rows, :] = partial[done + b * LANE : done + (b + 1) * LANE, :] + whiten(turned, b, wmat[...])
        put = pltpu.make_async_copy(
            last.at[rows, :], out.at[pl.ds(done + b * LANE, LANE), :], out_sem.at[ROUNDS - 1 + b]
        )
        put.start()
        puts.append(put)
    for put in puts:
        put.wait()


def on_device(raw, whitening, taps, temporal, spatial, spike_time, spike_template, spike_amp):
    bf16, f32 = jnp.bfloat16, jnp.float32
    whole = pl.BlockSpec(memory_space=pltpu.VMEM)
    far = pl.BlockSpec(memory_space=pltpu.HBM)
    samples = TCH * DEVICES
    arrays = tuple(pltpu.with_memory_space_constraint(array, pltpu.HBM) for array in (
        raw.reshape(CH, samples // LANE, LANE),
        whitening[0],
        taps[None],
        temporal,
        spatial[0],
        spike_time,
        spike_template,
        spike_amp,
    ))
    partial, late = pl.pallas_call(
        kernel,
        out_shape=(pltpu.VMEM((TCH, PCH), f32), pltpu.VMEM((DEVICES, ROWS, LANE), bf16)),
        in_specs=[far] * 8,
        out_specs=(whole, whole),
        scratch_shapes=[
            pltpu.VMEM((DEVICES, CH, 64, LANE), f32),
            pltpu.VMEM((ROUNDS, DEVICES, ROWS, LANE), bf16),
            pltpu.VMEM((ROUNDS - 1, DEVICES, ROWS, LANE), bf16),
            pltpu.VMEM((TCH // 4, NSP), bf16),
            pltpu.VMEM((NSP, NTEMP), bf16),
            pltpu.VMEM((TCH + 2 * HW, NTEMP), bf16),
            pltpu.VMEM((TCH + 2 * HW, RANK * PCH), bf16),
            pltpu.VMEM((DEVICES * ROWS, LANE), f32),
            pltpu.VMEM((256, 256), bf16),
            pltpu.VMEM((STEP, RANK * 256), bf16),
            pltpu.VMEM((PCH, PCH), bf16),
            pltpu.VMEM((RANK, NTEMP, PCH), bf16),
            pltpu.VMEM((1, NTAP), f32),
            pltpu.VMEM((RANK, NTAP), bf16),
            pltpu.VMEM((1, NSP), jnp.int32),
            pltpu.VMEM((1, NSP), jnp.int32),
            pltpu.VMEM((1, NSP), bf16),
            pltpu.VMEM((8, 256), f32),
            pltpu.VMEM((2, NSP // LANE, LANE), f32),
            pltpu.SemaphoreType.DMA((DEVICES,)),
            pltpu.SemaphoreType.DMA((7,)),
            pltpu.SemaphoreType.DMA((ROUNDS,)),
            pltpu.SemaphoreType.DMA((ROUNDS,)),
            pltpu.SemaphoreType.DMA((2,)),
            pltpu.SemaphoreType.DMA((2,)),
        ],
        compiler_params=pltpu.CompilerParams(
            collective_id=0, has_side_effects=True, vmem_limit_bytes=50 * 2**20
        ),
    )(*arrays)
    cleaned = pl.pallas_call(
        finish,
        out_shape=jax.ShapeDtypeStruct((TCH, PCH), f32),
        in_specs=[whole, whole, far],
        out_specs=far,
        scratch_shapes=[
            pltpu.VMEM((DEVICES * ROWS, LANE), f32),
            pltpu.VMEM((PCH, PCH), bf16),
            pltpu.VMEM((PER * LANE, PCH), f32),
            pltpu.SemaphoreType.DMA,
            pltpu.SemaphoreType.DMA((ROUNDS - 1 + PER,)),
        ],
        compiler_params=pltpu.CompilerParams(vmem_limit_bytes=16 * 2**20),
    )(
        pltpu.with_memory_space_constraint(partial, pltpu.VMEM),
        pltpu.with_memory_space_constraint(late, pltpu.VMEM),
        arrays[1],
    )
    return cleaned[None]


def solution(mesh):
    return jax.shard_map(
        on_device,
        mesh=mesh,
        in_specs=(
            P("probe", "tm", None),
            P("probe", None, None),
            P(),
            P(),
            P("probe", None, None, None),
            P("probe", "tm"),
            P("probe", "tm"),
            P("probe", "tm"),
        ),
        out_specs=P("probe", "tm", None),
        check_vma=False,
    )
```

```python
import jax
import jax.numpy as jnp
from jax import lax
from jax.experimental import pallas as pl
from jax.experimental.pallas import tpu as pltpu
from jax.sharding import PartitionSpec as P

MESH = pl.DeviceIdType.MESH
DEVICES = 32
CH = 12
PCH = 384
NTEMP = 256
RANK = 3
NTAP = 65
TCH = 4096
NSP = 2048
LANE = 128
BLOCKS = TCH // LANE
ROUNDS = 4
PER = BLOCKS // ROUNDS
ROWS = CH * PER
HW = 32
GROUP = 8
FIRST = 8
STEP = 192
MARGIN = 16


def hops(k):
    return k % 2 + min(k // 2 % 4, 4 - k // 2 % 4) + min(k // 8, 4 - k // 8)


ORDER = [(i * 11) % DEVICES for i in range(1, DEVICES + 1)]


def partner(me, k):
    x, y, z = me // 16, (me // 4) % 4, me % 4
    x = (x + k % 2) % 2
    y = (y + (k // 2) % 4) % 4
    z = (z + k // 8) % 4
    return x * 16 + y * 4 + z


def whiten(turned, b, wmat):
    block = turned[pl.ds(b, PCH, stride=PER), :].T.astype(jnp.bfloat16)
    return jnp.dot(block, wmat, preferred_element_type=jnp.float32)


def kernel(
    raw, white, taps, temporal, spatial, time, tmpl, amp, out, late,
    wide, outbox, inbox, hot, picked, events, loads, turned, band, bands, wmat, smat,
    taps_in, temporal_in, time_in, tmpl_in, amp_in, rows, lines,
    raw_sem, mat_sem, send_sem, recv_sem, halo_send, halo_recv,
):
    me = lax.axis_index("tm")

    small = ((taps, taps_in), (temporal, temporal_in), (time, time_in), (tmpl, tmpl_in), (amp, amp_in))
    gets = [
        pltpu.make_async_copy(there, here, mat_sem.at[i])
        for i, (there, here) in enumerate(small + ((spatial, smat), (white, wmat)))
    ]
    for get in gets[:2]:
        get.start()

    def fetch(i):
        to = partner(me, ORDER[i])
        start = 32 * to - 8 * ((to + 31) // 32) - 8 * ((to + 1) // 32)
        return pltpu.make_async_copy(
            raw.at[:, pl.ds(pl.multiple_of(start, 8), 48), :],
            wide.at[i, :, pl.ds(pl.multiple_of(start - 32 * to + MARGIN, 8), 48), :],
            raw_sem.at[i],
        )

    edge = jnp.zeros((CH, 8, LANE), jnp.float32)

    for i in range(FIRST):
        fetch(i).start()

    barrier = pltpu.get_barrier_semaphore()

    for k in ORDER[:-1]:
        pl.semaphore_signal(barrier, inc=1, device_id={"tm": partner(me, k)}, device_id_type=MESH)

    for i in range(DEVICES):
        if i >= FIRST:
            fetch(i).start()
        to = partner(me, ORDER[i])

        @pl.when(to == 0)
        def _(i=i):
            wide[i, :, MARGIN - 8 : MARGIN, :] = edge

        @pl.when(to == DEVICES - 1)
        def _(i=i):
            wide[i, :, MARGIN + BLOCKS : MARGIN + BLOCKS + 8, :] = edge

    for get in gets[2:]:
        get.start()

    rows[...] = jnp.zeros((8, 256), jnp.float32)
    gets[0].wait()
    rows[RANK : RANK + 1, 0:NTAP] = taps_in[...]

    fine = rows[RANK : RANK + 1, :]
    coarse = fine.astype(jnp.bfloat16).astype(jnp.float32)
    for i, part in enumerate((coarse, fine - coarse)):
        spread = jnp.broadcast_to(part, (LANE, 256))
        ring = pltpu.roll(spread, 224, 1, stride=1, stride_axis=0)
        band[:, i * LANE : (i + 1) * LANE] = ring.T.astype(jnp.bfloat16)

    def send(r, i):
        last = r == ROUNDS - 1
        pltpu.make_async_remote_copy(
            src_ref=outbox.at[r, i],
            dst_ref=late.at[me] if last else inbox.at[r, me],
            send_sem=send_sem.at[r],
            recv_sem=recv_sem.at[r],
            device_id={"tm": partner(me, ORDER[i])},
            device_id_type=MESH,
        ).start()

    def filter_group(r, at, count):
        slots, first = pl.ds(at, count), MARGIN + r * PER
        here = wide[slots, :, first : first + PER, :].reshape(count * ROWS, LANE)
        behind = wide[slots, :, first - 1 : first - 1 + PER, :].reshape(count * ROWS, LANE)
        ahead = wide[slots, :, first + 1 : first + 1 + PER, :].reshape(count * ROWS, LANE)
        lane = lax.broadcasted_iota(jnp.int32, here.shape, 1)
        beside = jnp.where(lane < 64, ahead, behind)
        both = jnp.dot(
            jnp.concatenate([here.astype(jnp.bfloat16), beside.astype(jnp.bfloat16)], axis=1),
            band[...], preferred_element_type=jnp.float32,
        )
        done = (both[:, :LANE] + both[:, LANE:]).astype(jnp.bfloat16)
        outbox[r, slots] = done.reshape(count, ROWS, LANE)

    def filter_and_send(r):
        @pl.loop(0, DEVICES // GROUP)
        def _(g):
            filter_group(r, g * GROUP, GROUP)

        for i in range(DEVICES - 1):
            send(r, i)
        (late if r == ROUNDS - 1 else inbox.at[r])[me] = outbox[r, DEVICES - 1]

    for i in range(0, DEVICES, FIRST):
        for j in range(i, i + FIRST):
            fetch(j).wait()
        filter_group(0, i, FIRST)
        if i == 0:
            pl.semaphore_wait(barrier, DEVICES - 1)
        for j in range(i, min(i + FIRST, DEVICES - 1)):
            send(0, j)
    inbox[0, me] = outbox[0, DEVICES - 1]
    filter_and_send(1)

    for get in gets[2:5]:
        get.wait()
    local = time_in[...] - me * TCH
    quarter = TCH // 4
    within = local % quarter
    code = (local // quarter) * NTEMP + tmpl_in[...]
    size = amp_in[...].astype(jnp.float32)
    for j in range(NSP // LANE):
        lines[0, j : j + 1, :] = code[:, j * LANE : (j + 1) * LANE].astype(jnp.float32)
        lines[1, j : j + 1, :] = size[:, j * LANE : (j + 1) * LANE]
    codes, sizes = lines[0].T, lines[1].T

    @pl.loop(0, quarter // 64)
    def _(i):
        row = lax.broadcasted_iota(jnp.int32, (64, NSP), 0) + i * 64
        hot[pl.ds(pl.multiple_of(i * 64, 64), 64), :] = jnp.where(row == within, 1.0, 0.0).astype(jnp.bfloat16)

    for q in range(4):
        column = (lax.broadcasted_iota(jnp.int32, (LANE, NTEMP), 1) + q * NTEMP).astype(jnp.float32)
        for j in range(NSP // LANE):
            mine = jnp.where(column == codes[:, j : j + 1], sizes[:, j : j + 1], 0.0)
            picked[j * LANE : (j + 1) * LANE, :] = mine.astype(jnp.bfloat16)

        @pl.loop(0, quarter // 256)
        def _(m):
            total = jnp.dot(
                hot[pl.ds(pl.multiple_of(m * 256, 256), 256), :], picked[...],
                preferred_element_type=jnp.float32,
            )
            at = pl.multiple_of(HW + q * quarter + m * 256, 32)
            events[pl.ds(at, 256), :] = total.astype(jnp.bfloat16)

    def to_next():
        return pltpu.make_async_remote_copy(
            src_ref=events.at[pl.ds(TCH, HW), :],
            dst_ref=events.at[pl.ds(0, HW), :],
            send_sem=halo_send.at[0],
            recv_sem=halo_recv.at[0],
            device_id={"tm": (me + 1) % DEVICES},
            device_id_type=MESH,
        )

    def to_prev():
        return pltpu.make_async_remote_copy(
            src_ref=events.at[pl.ds(HW, HW), :],
            dst_ref=events.at[pl.ds(TCH + HW, HW), :],
            send_sem=halo_send.at[1],
            recv_sem=halo_recv.at[1],
            device_id={"tm": (me + DEVICES - 1) % DEVICES},
            device_id_type=MESH,
        )

    none = jnp.zeros((HW, NTEMP), jnp.bfloat16)

    @pl.when(me == 0)
    def _():
        events[0:HW, :] = none

    @pl.when(me == DEVICES - 1)
    def _():
        events[TCH + HW : TCH + 2 * HW, :] = none

    @pl.when(me < DEVICES - 1)
    def _():
        to_next().start()

    @pl.when(me > 0)
    def _():
        to_prev().start()

    filter_and_send(2)
    filter_and_send(3)

    gets[5].wait()

    def load_rows(at, count):
        part = events[pl.ds(at, count), :]
        for r in range(RANK):
            value = jnp.dot(part, smat[r], preferred_element_type=jnp.float32)
            loads[pl.ds(at, count), r * PCH : (r + 1) * PCH] = value.astype(jnp.bfloat16)

    @pl.loop(0, TCH // 256)
    def _(i):
        load_rows(pl.multiple_of(HW + i * 256, 32), 256)

    gets[1].wait()
    rows[0:RANK, 0:NTAP] = temporal_in[...].astype(jnp.float32)

    for r in range(RANK):
        spread = jnp.broadcast_to(-rows[r : r + 1, :], (256, 256))
        ring = pltpu.roll(spread, 192, 1, stride=1, stride_axis=0)
        bands[:, r * 256 : (r + 1) * 256] = ring.T[:STEP].astype(jnp.bfloat16)

    @pl.when(me > 0)
    def _():
        to_next().wait_recv()

    @pl.when(me < DEVICES - 1)
    def _():
        to_prev().wait_recv()

    load_rows(0, HW)
    load_rows(TCH + HW, HW)

    def spill(at):
        part = jnp.concatenate([loads[pl.ds(at, 256), r * PCH : (r + 1) * PCH] for r in range(RANK)], axis=0)
        out[pl.ds(at, STEP), :] = jnp.dot(bands[...], part, preferred_element_type=jnp.float32)

    @pl.loop(0, TCH // STEP // 3)
    def _(i):
        for j in range(3):
            spill(pl.multiple_of(i * (3 * STEP) + j * STEP, 64))

    spill(TCH - STEP)

    gets[6].wait()
    several = pl.ds(0, DEVICES - 1)

    @pl.loop(0, ROUNDS - 1)
    def _(r):
        pltpu.make_async_copy(outbox.at[r, several], inbox.at[r, several], recv_sem.at[r]).wait()
        turned[...] = inbox[r].reshape(DEVICES * ROWS, LANE).astype(jnp.float32)
        for b in range(PER):
            at = pl.ds(pl.multiple_of((r * PER + b) * LANE, LANE), LANE)
            out[at, :] = out[at, :] + whiten(turned, b, wmat[...])

    r = ROUNDS - 1
    pltpu.make_async_copy(outbox.at[r, several], late.at[several], recv_sem.at[r]).wait()
    for r in range(ROUNDS):
        pltpu.make_async_copy(outbox.at[r, several], outbox.at[r, several], send_sem.at[r]).wait()

    @pl.when(me < DEVICES - 1)
    def _():
        to_next().wait_send()

    @pl.when(me > 0)
    def _():
        to_prev().wait_send()


def finish(partial, late, white, out, turned, wmat, last, mat_sem, out_sem):
    get = pltpu.make_async_copy(white, wmat, mat_sem)
    get.start()
    done = (ROUNDS - 1) * PER * LANE
    puts = []
    for i in range(ROUNDS - 1):
        at = pl.ds(i * PER * LANE, PER * LANE)
        puts.append(pltpu.make_async_copy(partial.at[at, :], out.at[at, :], out_sem.at[i]))
    for put in puts:
        put.start()
    turned[...] = late[...].reshape(DEVICES * ROWS, LANE).astype(jnp.float32)
    get.wait()
    for b in range(PER):
        rows = pl.ds(b * LANE, LANE)
        last[rows, :] = partial[done + b * LANE : done + (b + 1) * LANE, :] + whiten(turned, b, wmat[...])
        put = pltpu.make_async_copy(
            last.at[rows, :], out.at[pl.ds(done + b * LANE, LANE), :], out_sem.at[ROUNDS - 1 + b]
        )
        put.start()
        puts.append(put)
    for put in puts:
        put.wait()


def on_device(raw, whitening, taps, temporal, spatial, spike_time, spike_template, spike_amp):
    bf16, f32 = jnp.bfloat16, jnp.float32
    whole = pl.BlockSpec(memory_space=pltpu.VMEM)
    far = pl.BlockSpec(memory_space=pltpu.HBM)
    samples = TCH * DEVICES
    arrays = tuple(pltpu.with_memory_space_constraint(array, pltpu.HBM) for array in (
        raw.reshape(CH, samples // LANE, LANE),
        whitening[0],
        taps[None],
        temporal,
        spatial[0],
        spike_time,
        spike_template,
        spike_amp,
    ))
    partial, late = pl.pallas_call(
        kernel,
        out_shape=(pltpu.VMEM((TCH, PCH), f32), pltpu.VMEM((DEVICES, ROWS, LANE), bf16)),
        in_specs=[far] * 8,
        out_specs=(whole, whole),
        scratch_shapes=[
            pltpu.VMEM((DEVICES, CH, 64, LANE), f32),
            pltpu.VMEM((ROUNDS, DEVICES, ROWS, LANE), bf16),
            pltpu.VMEM((ROUNDS - 1, DEVICES, ROWS, LANE), bf16),
            pltpu.VMEM((TCH // 4, NSP), bf16),
            pltpu.VMEM((NSP, NTEMP), bf16),
            pltpu.VMEM((TCH + 2 * HW, NTEMP), bf16),
            pltpu.VMEM((TCH + 2 * HW, RANK * PCH), bf16),
            pltpu.VMEM((DEVICES * ROWS, LANE), f32),
            pltpu.VMEM((256, 256), bf16),
            pltpu.VMEM((STEP, RANK * 256), bf16),
            pltpu.VMEM((PCH, PCH), bf16),
            pltpu.VMEM((RANK, NTEMP, PCH), bf16),
            pltpu.VMEM((1, NTAP), f32),
            pltpu.VMEM((RANK, NTAP), bf16),
            pltpu.VMEM((1, NSP), jnp.int32),
            pltpu.VMEM((1, NSP), jnp.int32),
            pltpu.VMEM((1, NSP), bf16),
            pltpu.VMEM((8, 256), f32),
            pltpu.VMEM((2, NSP // LANE, LANE), f32),
            pltpu.SemaphoreType.DMA((DEVICES,)),
            pltpu.SemaphoreType.DMA((7,)),
            pltpu.SemaphoreType.DMA((ROUNDS,)),
            pltpu.SemaphoreType.DMA((ROUNDS,)),
            pltpu.SemaphoreType.DMA((2,)),
            pltpu.SemaphoreType.DMA((2,)),
        ],
        compiler_params=pltpu.CompilerParams(
            collective_id=0, has_side_effects=True, vmem_limit_bytes=50 * 2**20
        ),
    )(*arrays)
    cleaned = pl.pallas_call(
        finish,
        out_shape=jax.ShapeDtypeStruct((TCH, PCH), f32),
        in_specs=[whole, whole, far],
        out_specs=far,
        scratch_shapes=[
            pltpu.VMEM((DEVICES * ROWS, LANE), f32),
            pltpu.VMEM((PCH, PCH), bf16),
            pltpu.VMEM((PER * LANE, PCH), f32),
            pltpu.SemaphoreType.DMA,
            pltpu.SemaphoreType.DMA((ROUNDS - 1 + PER,)),
        ],
        compiler_params=pltpu.CompilerParams(vmem_limit_bytes=16 * 2**20),
    )(
        pltpu.with_memory_space_constraint(partial, pltpu.VMEM),
        pltpu.with_memory_space_constraint(late, pltpu.VMEM),
        arrays[1],
    )
    return cleaned[None]


def solution(mesh):
    return jax.shard_map(
        on_device,
        mesh=mesh,
        in_specs=(
            P("probe", "tm", None),
            P("probe", None, None),
            P(),
            P(),
            P("probe", None, None, None),
            P("probe", "tm"),
            P("probe", "tm"),
            P("probe", "tm"),
        ),
        out_specs=P("probe", "tm", None),
        check_vma=False,
    )
```
